32 devices in a mesh: seq: 16 (over z, y, core), head: 2 (over x).
Axes of the slice: x: 2, y: 2, z: 4, core: 2. Of those that a mesh axis runs over, the one named last changes fastest.
Arguments:
- embedded: bfloat16 [4096, 1536], P('seq', 'head'), may hold values from -27 to 27
- grad_out: bfloat16 [4096, 1536], P('seq', 'head'), may hold values from -6 to 6
- mask_pos: int32 [608], P('seq'), may hold values from 0 to 4095, as said below
- timestep: int32 [1], replicated, may hold values from 0 to 999
- time_table: bfloat16 [1000, 1536], replicated, may hold values from -3 to 3
- mask_embed: bfloat16 [1536], replicated, may hold values from -6 to 6
- w_query: bfloat16 [1536, 768], P(None, 'head'), may hold values from -0.15625 to 0.15625
- w_key: bfloat16 [1536, 768], P(None, 'head'), may hold values from -0.15625 to 0.15625
- w_value: bfloat16 [1536, 768], P(None, 'head'), may hold values from -0.15625 to 0.15625
- w_out: bfloat16 [768, 1536], P('head'), may hold values from -0.21875 to 0.21875
Outputs:
- input_grad: bfloat16 [4096, 1536], P('seq', 'head')
- query_weight_grad: float32 [1536, 768], P('seq', 'head')
- key_weight_grad: float32 [1536, 768], P('seq', 'head')
- value_weight_grad: float32 [1536, 768], P('seq', 'head')
- out_weight_grad: float32 [1536, 768], P('seq', 'head')
The draws below stay inside these ranges and needn't reach their ends.
Inputs may be any that keep to these rules, and one draw needn't show every extreme that they name: `mask_pos`: the entries are distinct; entries b * 38 to (b + 1) * 38 - 1 lie in positions b * 256 to (b + 1) * 256 - 1.
All inputs are finite; a program needn't handle non-finite values.
Results may differ from the reference program's by a relative error of at most 0.01.
The reference program's roundings to bfloat16 on the way count: a program that leaves them out, or rounds other values in their place, can miss the bound.
Values may be sent and summed in bfloat16 or wider, within the bound.
A program may use at most 128 MiB of HBM per device.

```python
import jax
import jax.numpy as jnp
from jax import lax

D = 1536
HEADS = 12
HEAD_DIM = 64
HALF = 1024
TSTEPS = 1000
S_DEV = 256
MASK_DEV = 38
SEQ_LEN = 4096


def draw_embedded(key, part):
    base = jax.random.normal(jax.random.fold_in(key, 1), (SEQ_LEN, D), jnp.float32)
    base = jnp.clip(base, -6.0, 6.0)
    return base.astype(jnp.bfloat16)


def draw_mask_pos(key, part):
    blocks = SEQ_LEN // S_DEV
    block_keys = jax.random.split(key, blocks)
    chosen = jax.vmap(lambda one_key: jax.random.permutation(one_key, S_DEV)[:MASK_DEV])(block_keys)
    offsets = jnp.arange(blocks, dtype=jnp.int32)[:, None] * S_DEV
    return (chosen.astype(jnp.int32) + offsets).reshape(-1)


def strengthened(values, stream_key, source, target, parts, factor):
    owner, partner = [(jnp.arange(values.shape[position]) // (values.shape[position] // parts)).reshape([-1 if axis == position else 1 for axis in range(values.ndim)]) for position in (source, target)]
    chosen = jax.random.permutation(stream_key, parts)[partner]
    strong = (owner == chosen) | (owner == (partner + parts // 2) % parts)
    return jnp.where(strong, factor * values, values)


def block_scale(stream_key, dims, cuts, smallest, high):
    factor_of = 1.0
    for dim, blocks in cuts:
        heights = jax.random.uniform(jax.random.fold_in(jax.random.fold_in(stream_key, 6), dim), (blocks,), jnp.float32, smallest / len(cuts), high / len(cuts))
        factor_of = factor_of * jnp.repeat(jnp.exp(heights), dims[dim] // blocks).reshape((-1,) + (1,) * (len(dims) - 1 - dim))
    return factor_of


def noise(rng, dims, spread, reach, pieces=(), kind=jnp.bfloat16):
    entries = spread * jax.random.normal(rng, dims, jnp.float32)
    if pieces:
        entries = entries * block_scale(rng, dims, pieces, -0.22, 0.18)
    return jnp.clip(entries, -reach, reach).astype(kind)


def gaussian_with(stream_key, extent, spread, bound, shards, heavy, held_as=jnp.bfloat16):
    array = spread * jax.random.normal(stream_key, extent, jnp.float32)
    if shards:
        array = array * block_scale(stream_key, extent, shards, -0.22, 0.18)
    return jnp.clip(strengthened(array, jax.random.fold_in(stream_key, 3), *heavy), -bound, bound).astype(held_as)


def setup_inputs(seed: int = 0) -> dict:
    key_list = jax.random.split(jax.random.key(seed), 11)
    return {
        "embedded": draw_embedded(jax.random.fold_in(key_list[10], 71), 0),
        "grad_out": gaussian_with(key_list[1], (SEQ_LEN, D), 1.0, 6.0, ((0, 16), (1, 2)), (0, 1, 16, 2.0)),
        "mask_pos": draw_mask_pos(jax.random.fold_in(key_list[10], 71), 0),
        "timestep": jax.random.randint(key_list[3], (1,), 0, TSTEPS).astype(jnp.int32),
        "time_table": noise(key_list[4], (TSTEPS, D), 0.5, 3.0),
        "mask_embed": noise(key_list[5], (D,), 1.0, 6.0),
        "w_query": noise(key_list[6], (D, HEADS * HEAD_DIM), D ** -0.5, 0.15625, ((1, 2),)),
        "w_key": noise(key_list[7], (D, HEADS * HEAD_DIM), D ** -0.5, 0.15625, ((1, 2),)),
        "w_value": noise(key_list[8], (D, HEADS * HEAD_DIM), D ** -0.5, 0.15625, ((1, 2),)),
        "w_out": noise(key_list[9], (HEADS * HEAD_DIM, D), (HEADS * HEAD_DIM) ** -0.5, 0.21875, ((0, 2),)),
    }


NEG_FILL = -1.0e30


def reference(embedded, grad_out, mask_pos, timestep, time_table, mask_embed, w_query, w_key, w_value, w_out):
    width = HEADS * HEAD_DIM
    scale = HEAD_DIM ** -0.5
    masked = jnp.zeros((SEQ_LEN,), jnp.float32).at[mask_pos].set(1.0) > 0.5
    time_row = lax.dynamic_slice_in_dim(time_table, timestep[0], 1, 0).astype(jnp.float32)
    hidden = (jnp.where(masked[:, None], mask_embed.astype(jnp.float32)[None, :], embedded.astype(jnp.float32)) + time_row).astype(jnp.bfloat16)
    queries = jnp.dot(hidden, w_query, preferred_element_type=jnp.float32).astype(jnp.bfloat16)
    key_rows = jnp.dot(hidden, w_key, preferred_element_type=jnp.float32).astype(jnp.bfloat16)
    value_rows = jnp.dot(hidden, w_value, preferred_element_type=jnp.float32).astype(jnp.bfloat16)
    grad_attn = jnp.dot(grad_out, w_out.T, preferred_element_type=jnp.float32).astype(jnp.bfloat16)
    key_pad = jnp.pad(key_rows, ((HALF, HALF), (0, 0)))
    value_pad = jnp.pad(value_rows, ((HALF, HALF), (0, 0)))
    span = S_DEV + 2 * HALF

    def step_block(carry, block_index):
        key_grad_pad, value_grad_pad = carry
        start = (block_index * S_DEV).astype(jnp.int32)
        query_block = lax.dynamic_slice_in_dim(queries, start, S_DEV, 0).astype(jnp.float32).reshape(S_DEV, HEADS, HEAD_DIM)
        grad_block = lax.dynamic_slice_in_dim(grad_attn, start, S_DEV, 0).astype(jnp.float32).reshape(S_DEV, HEADS, HEAD_DIM)
        key_block = lax.dynamic_slice_in_dim(key_pad, start, span, 0).astype(jnp.float32).reshape(span, HEADS, HEAD_DIM)
        value_block = lax.dynamic_slice_in_dim(value_pad, start, span, 0).astype(jnp.float32).reshape(span, HEADS, HEAD_DIM)
        query_pos = start + jnp.arange(S_DEV, dtype=jnp.int32)
        key_pos = start - HALF + jnp.arange(span, dtype=jnp.int32)
        distance = query_pos[:, None] - key_pos[None, :]
        band = (jnp.abs(distance) <= HALF) & (key_pos[None, :] >= 0) & (key_pos[None, :] < SEQ_LEN)
        scores = jnp.einsum("qhe,khe->hqk", query_block, key_block) * scale
        scores = jnp.where(band[None], scores, NEG_FILL)
        row_max = jnp.max(scores, axis=2, keepdims=True)
        log_total = row_max + jnp.log(jnp.sum(jnp.exp(scores - row_max), axis=2, keepdims=True))
        attention = jnp.exp(scores - log_total)
        rounded = lax.optimization_barrier(attention.astype(jnp.bfloat16)).astype(jnp.float32)
        outputs = jnp.einsum("hqk,khe->qhe", rounded, value_block).astype(jnp.bfloat16)
        out_wide = lax.optimization_barrier(outputs).astype(jnp.float32)
        delta = jnp.einsum("qhe,qhe->hq", grad_block, out_wide)
        dprob = jnp.einsum("qhe,khe->hqk", grad_block, value_block)
        dscore = lax.optimization_barrier((attention * (dprob - delta[:, :, None])).astype(jnp.bfloat16)).astype(jnp.float32)
        query_grad = scale * jnp.einsum("hqk,khe->qhe", dscore, key_block)
        key_grad = scale * jnp.einsum("hqk,qhe->khe", dscore, query_block)
        value_grad = jnp.einsum("hqk,qhe->khe", rounded, grad_block)
        old_keys = lax.dynamic_slice_in_dim(key_grad_pad, start, span, 0)
        old_values = lax.dynamic_slice_in_dim(value_grad_pad, start, span, 0)
        key_grad_pad = lax.dynamic_update_slice_in_dim(key_grad_pad, old_keys + key_grad.reshape(span, width), start, 0)
        value_grad_pad = lax.dynamic_update_slice_in_dim(value_grad_pad, old_values + value_grad.reshape(span, width), start, 0)
        return (key_grad_pad, value_grad_pad), (outputs.reshape(S_DEV, width), query_grad.reshape(S_DEV, width))

    start_pads = (jnp.zeros((SEQ_LEN + 2 * HALF, width), jnp.float32), jnp.zeros((SEQ_LEN + 2 * HALF, width), jnp.float32))
    (key_grad_pad, value_grad_pad), (attn_out, query_grad) = lax.scan(step_block, start_pads, jnp.arange(SEQ_LEN // S_DEV, dtype=jnp.int32))
    attn_out = attn_out.reshape(SEQ_LEN, width)
    query_rounded = query_grad.reshape(SEQ_LEN, width).astype(jnp.bfloat16)
    key_rounded = key_grad_pad[HALF:HALF + SEQ_LEN].astype(jnp.bfloat16)
    value_rounded = value_grad_pad[HALF:HALF + SEQ_LEN].astype(jnp.bfloat16)
    query_weight_grad = jnp.dot(hidden.T, query_rounded, preferred_element_type=jnp.float32)
    key_weight_grad = jnp.dot(hidden.T, key_rounded, preferred_element_type=jnp.float32)
    value_weight_grad = jnp.dot(hidden.T, value_rounded, preferred_element_type=jnp.float32)
    out_weight_grad = jnp.dot(grad_out.T, attn_out, preferred_element_type=jnp.float32)
    summed = jnp.dot(query_rounded, w_query.T, preferred_element_type=jnp.float32)
    summed = summed + jnp.dot(key_rounded, w_key.T, preferred_element_type=jnp.float32)
    summed = summed + jnp.dot(value_rounded, w_value.T, preferred_element_type=jnp.float32)
    input_grad = jnp.where(masked[:, None], 0.0, summed).astype(jnp.bfloat16)
    return (input_grad, query_weight_grad, key_weight_grad, value_weight_grad, out_weight_grad)
```

```python
import jax
import jax.numpy as jnp
from jax import lax
from jax.sharding import PartitionSpec as P

HEAD_DIM = 64
HALF = 1024


NEG_FILL = -1e30


def contract_first(left, right):
    return lax.dot_general(
        left, right, (((0,), (0,)), ((), ())), preferred_element_type=jnp.float32
    )


def contract_last(left, right):
    return lax.dot_general(
        left, right, (((1,), (1,)), ((), ())), preferred_element_type=jnp.float32
    )


def swapped(value, axis, bit):
    count = lax.axis_size(axis)
    return lax.ppermute(value, axis, [(source, source ^ bit) for source in range(count)])


def passed_along(value, axis, steps):
    count = lax.axis_size(axis)
    first, last = (max(0, -steps), min(count, count - steps))
    return lax.ppermute(value, axis, [(source, source + steps) for source in range(first, last)])


def picked(array, index, axis):
    return lax.dynamic_index_in_dim(array, index, axis, keepdims=False)


def joined_heads(mine, head_index):
    other = swapped(mine, "head", 1)
    first = jnp.where(head_index == 0, mine, other)
    second = jnp.where(head_index == 0, other, mine)
    return jnp.concatenate([first, second], axis=1)


def summed_rows(part, seq_index):
    count = lax.axis_size("seq")
    groups = count // 4
    rows = part.shape[0] // count
    width = part.shape[1]
    core, side, group = seq_index % 2, seq_index // 2 % 2, seq_index // 4
    blocks = part.reshape(groups, 2, 2, rows, width)
    blocks = picked(blocks, core, 2) + swapped(picked(blocks, 1 - core, 2), "seq", 1)
    sent = picked(blocks, 1 - side, 1).astype(jnp.bfloat16)
    blocks = picked(blocks, side, 1) + swapped(sent, "seq", 2).astype(jnp.float32)
    if groups > 4:
        members = [[g * 4 + place for g in range(groups)] for place in range(4)]
        return lax.psum_scatter(
            blocks.reshape(groups * rows, width),
            "seq",
            scatter_dimension=0,
            axis_index_groups=members,
            tiled=True,
        )
    narrow = blocks.astype(jnp.bfloat16)
    total = picked(blocks, group, 0)
    for distance in range(1, groups):
        for step in (distance, -distance):
            target = jnp.clip(group + step, 0, groups - 1)
            arrived = passed_along(picked(narrow, target, 0), "seq", 4 * step)
            total = total + arrived.astype(jnp.float32)
    return total


def body(
    embedded, grad_out, mask_pos, timestep, time_table, mask_embed, w_query, w_key, w_value, w_out
):
    seq_index = lax.axis_index("seq")
    seq_count = lax.axis_size("seq")
    head_place = lax.axis_index("head")
    core, side = seq_index % 2, seq_index // 2 % 2
    slab_rows = embedded.shape[0]
    total_len = slab_rows * seq_count
    scale = HEAD_DIM ** (-0.5)
    full_rows = joined_heads(embedded, head_place)
    full_grad = joined_heads(grad_out, head_place)
    positions = seq_index * slab_rows + jnp.arange(slab_rows, dtype=jnp.int32)
    masked = jnp.any(positions[:, None] == mask_pos[None, :], axis=1)
    time_row = lax.dynamic_slice_in_dim(time_table, timestep[0], 1, 0).astype(jnp.float32)
    hidden = (
        jnp.where(
            masked[:, None], mask_embed.astype(jnp.float32)[None, :], full_rows.astype(jnp.float32)
        )
        + time_row
    ).astype(jnp.bfloat16)
    key_rows = jnp.dot(hidden, w_key, preferred_element_type=jnp.float32).astype(jnp.bfloat16)
    value_rows = jnp.dot(hidden, w_value, preferred_element_type=jnp.float32).astype(jnp.bfloat16)
    queries = jnp.dot(hidden, w_query, preferred_element_type=jnp.float32).astype(jnp.bfloat16)
    grad_attn = contract_last(full_grad, w_out).astype(jnp.bfloat16)
    group_width = queries.shape[1]
    head_count = group_width // HEAD_DIM

    own = jnp.concatenate([key_rows, value_rows], axis=1)
    below = passed_along(own, "seq", 4)
    above = passed_along(own, "seq", -4)
    plane_side = swapped(own, "seq", 2)
    plane_core = swapped(own, "seq", 1)
    far_side = swapped(jnp.where(side == 1, below, above), "seq", 2)
    far_core = swapped(jnp.where(core == 1, below, above), "seq", 1)
    plane_both = swapped(plane_side, "seq", 1)
    far_both = swapped(far_side, "seq", 1)
    slabs = jnp.concatenate(
        [far_both, plane_both, far_core, plane_core, far_side, plane_side, own, below, above],
        axis=0,
    )
    core_step = 4 - 8 * (1 - core)
    side_step = 4 - 8 * (1 - side)
    numbers = [
        (seq_index ^ 3) + side_step,
        seq_index ^ 3,
        (seq_index ^ 1) + core_step,
        seq_index ^ 1,
        (seq_index ^ 2) + side_step,
        seq_index ^ 2,
        seq_index,
        seq_index - 4,
        seq_index + 4,
    ]
    offsets = jnp.arange(slab_rows, dtype=jnp.int32)
    key_pos = jnp.concatenate([number * slab_rows + offsets for number in numbers])
    keys_all = slabs[:, :group_width]
    values_all = slabs[:, group_width:]
    distance_grid = positions[:, None] - key_pos[None, :]
    band = (
        (jnp.abs(distance_grid) <= HALF) & (key_pos[None, :] >= 0) & (key_pos[None, :] < total_len)
    )
    head_outputs = []
    query_grads = []
    key_grads = []
    value_grads = []
    for head_index in range(head_count):
        lower_col = head_index * HEAD_DIM
        upper_col = lower_col + HEAD_DIM
        head_query = queries[:, lower_col:upper_col]
        head_keys = keys_all[:, lower_col:upper_col]
        head_values = values_all[:, lower_col:upper_col]
        head_grad = grad_attn[:, lower_col:upper_col]
        scores = contract_last(head_query, head_keys) * scale
        scores = jnp.where(band, scores, NEG_FILL)
        row_max = jnp.max(scores, axis=1, keepdims=True)
        log_total = row_max + jnp.log(jnp.sum(jnp.exp(scores - row_max), axis=1, keepdims=True))
        attention = jnp.exp(scores - log_total)
        rounded = attention.astype(jnp.bfloat16)
        output = jnp.dot(rounded, head_values, preferred_element_type=jnp.float32).astype(
            jnp.bfloat16
        )
        head_outputs.append(output)
        delta = jnp.sum(head_grad.astype(jnp.float32) * output.astype(jnp.float32), axis=1)
        dprob = contract_last(head_grad, head_values)
        dscore = (attention * (dprob - delta[:, None])).astype(jnp.bfloat16)
        query_grads.append(scale * jnp.dot(dscore, head_keys, preferred_element_type=jnp.float32))
        key_grads.append(scale * contract_first(dscore, head_query))
        value_grads.append(contract_first(rounded, head_grad))
    attn_out = jnp.concatenate(head_outputs, axis=1)
    query_rounded = jnp.concatenate(query_grads, axis=1).astype(jnp.bfloat16)
    slab_grads = jnp.concatenate(key_grads + value_grads, axis=1)

    def slab_of(first, count):
        return slab_grads[first * slab_rows : (first + count) * slab_rows]

    by_core = swapped(slab_of(0, 4), "seq", 1)
    for_side = by_core[: 2 * slab_rows] + slab_of(4, 2)
    by_side = swapped(for_side, "seq", 2).astype(jnp.float32)
    core_far, core_own = by_core[2 * slab_rows : 3 * slab_rows], by_core[3 * slab_rows :]
    side_far, side_own = by_side[:slab_rows], by_side[slab_rows:]
    to_below = slab_of(7, 1) + jnp.where(core == 1, core_far, 0.0) + jnp.where(side == 1, side_far, 0.0)
    to_above = slab_of(8, 1) + jnp.where(core == 0, core_far, 0.0) + jnp.where(side == 0, side_far, 0.0)
    slab_total = slab_of(6, 1) + core_own + side_own
    slab_total = slab_total + passed_along(to_below, "seq", -4).astype(jnp.float32)
    slab_total = slab_total + passed_along(to_above, "seq", 4).astype(jnp.float32)
    pair_rounded = slab_total.astype(jnp.bfloat16)

    early = summed_rows(
        jnp.concatenate(
            [contract_first(hidden, query_rounded), contract_first(full_grad, attn_out)], axis=1
        ),
        seq_index,
    )
    late = summed_rows(contract_first(hidden, pair_rounded), seq_index)
    partial_grad = contract_last(query_rounded, w_query)
    partial_grad = partial_grad + contract_last(pair_rounded[:, :group_width], w_key)
    partial_grad = partial_grad + contract_last(pair_rounded[:, group_width:], w_value)
    half = embedded.shape[1]
    left, right = partial_grad[:, :half], partial_grad[:, half:]
    kept = jnp.where(head_place == 0, left, right)
    summed = kept + swapped(jnp.where(head_place == 0, right, left), "head", 1)
    input_grad = jnp.where(masked[:, None], 0.0, summed).astype(jnp.bfloat16)
    return (
        input_grad,
        early[:, :group_width],
        late[:, :group_width],
        late[:, group_width:],
        early[:, group_width:],
    )


def solution(mesh):
    placed = (
        P("seq", "head"),
        P("seq", "head"),
        P("seq"),
        P(),
        P(),
        P(),
        P(None, "head"),
        P(None, "head"),
        P(None, "head"),
        P("head", None),
    )
    return jax.shard_map(
        body,
        mesh=mesh,
        in_specs=placed,
        out_specs=(
            P("seq", "head"),
            P("seq", "head"),
            P("seq", "head"),
            P("seq", "head"),
            P("seq", "head"),
        ),
        check_vma=False,
    )
```

```python
import functools

import jax
import jax.numpy as jnp
from jax import lax
from jax.experimental import pallas as pl
from jax.experimental.pallas import tpu as pltpu
from jax.sharding import PartitionSpec as P

HEAD_DIM = 64
HALF = 1024


NEG_FILL = -1e30


def contract_first(left, right):
    return lax.dot_general(
        left, right, (((0,), (0,)), ((), ())), preferred_element_type=jnp.float32
    )


def contract_last(left, right):
    return lax.dot_general(
        left, right, (((1,), (1,)), ((), ())), preferred_element_type=jnp.float32
    )


def swapped(value, axis, bit):
    count = lax.axis_size(axis)
    return lax.ppermute(value, axis, [(source, source ^ bit) for source in range(count)])


def passed_along(value, axis, steps):
    count = lax.axis_size(axis)
    first, last = (max(0, -steps), min(count, count - steps))
    return lax.ppermute(value, axis, [(source, source + steps) for source in range(first, last)])


def picked(array, index, axis):
    return lax.dynamic_index_in_dim(array, index, axis, keepdims=False)


def joined_heads(mine, head_index):
    other = swapped(mine, "head", 1)
    first = jnp.where(head_index == 0, mine, other)
    second = jnp.where(head_index == 0, other, mine)
    return jnp.concatenate([first, second], axis=1)


def core_summed(part, seq_index):
    count = lax.axis_size("seq")
    core = seq_index % 2
    blocks = part.reshape(count // 4, 2, 2, part.shape[0] // count, part.shape[1])
    return picked(blocks, core, 2) + swapped(picked(blocks, 1 - core, 2), "seq", 1)


def side_summed(blocks, seq_index):
    side = seq_index // 2 % 2
    sent = picked(blocks, 1 - side, 1).astype(jnp.bfloat16)
    return picked(blocks, side, 1) + swapped(sent, "seq", 2).astype(jnp.float32)


def group_summed(blocks):
    groups, rows, width = blocks.shape
    members = [[g * 4 + place for g in range(groups)] for place in range(4)]
    return lax.psum_scatter(
        blocks.reshape(groups * rows, width),
        "seq",
        scatter_dimension=0,
        axis_index_groups=members,
        tiled=True,
    )


def closing_kernel(
    groups,
    early_ref,
    late_ref,
    kept_ref,
    sent_ref,
    early_out,
    late_out,
    summed_out,
    early_send,
    early_slots,
    core_slot,
    side_send,
    side_slot,
    total,
    late_send,
    late_slots,
    head_slot,
    single_send,
    single_recv,
    early_send_sems,
    early_recv_sems,
    late_send_sems,
    late_recv_sems,
):
    me = lax.axis_index("seq")
    head = lax.axis_index("head")
    core = lax.rem(me, 2)
    side = lax.rem(me // 2, 2)
    group = me // 4
    place = lax.rem(me, 4)
    core_peer = me + 1 - 2 * core
    side_peer = me + 2 - 4 * side
    targets = [lax.rem(group + step, groups) for step in range(1, groups)]
    peers = [(core_peer, head), (side_peer, head), (me, 1 - head)]
    peers += [(target * 4 + place, head) for target in targets]

    barrier = pltpu.get_barrier_semaphore()
    for peer in peers:
        pl.semaphore_signal(barrier, inc=1, device_id=peer, device_id_type=pl.DeviceIdType.MESH)
    pl.semaphore_wait(barrier, len(peers))

    def remote(source, target, send, recv, peer):
        copy = pltpu.make_async_remote_copy(
            src_ref=source,
            dst_ref=target,
            send_sem=send,
            recv_sem=recv,
            device_id=peer,
            device_id_type=pl.DeviceIdType.MESH,
        )
        copy.start()
        return copy

    core_copy = remote(
        late_ref.at[1 - core], core_slot, single_send.at[0], single_recv.at[0], peers[0]
    )
    early_send[...] = early_ref[...].astype(jnp.bfloat16)
    early_copies = []
    for step in range(1, groups):
        early_copies.append(
            remote(
                early_send.at[targets[step - 1]],
                early_slots.at[step - 1],
                early_send_sems.at[step - 1],
                early_recv_sems.at[step - 1],
                peers[2 + step],
            )
        )
    head_copy = remote(sent_ref, head_slot, single_send.at[2], single_recv.at[2], peers[2])
    core_copy.wait()
    side_send[...] = (late_ref[core, 1 - side] + core_slot[1 - side]).astype(jnp.bfloat16)
    side_copy = remote(side_send, side_slot, single_send.at[1], single_recv.at[1], peers[1])
    total[...] = late_ref[core, side] + core_slot[side]
    side_copy.wait()
    total[...] = total[...] + side_slot[...].astype(jnp.float32)
    late_send[...] = total[...].astype(jnp.bfloat16)
    late_copies = []
    for step in range(1, groups):
        late_copies.append(
            remote(
                late_send.at[targets[step - 1]],
                late_slots.at[step - 1],
                late_send_sems.at[step - 1],
                late_recv_sems.at[step - 1],
                peers[2 + step],
            )
        )
    head_copy.wait()
    summed_out[...] = kept_ref[...] + head_slot[...]
    result = early_ref[group]
    for step in range(1, groups):
        early_copies[step - 1].wait()
        result = result + early_slots[step - 1].astype(jnp.float32)
    early_out[...] = result
    result = total[group]
    for step in range(1, groups):
        late_copies[step - 1].wait()
        result = result + late_slots[step - 1].astype(jnp.float32)
    late_out[...] = result


def closing_sums(early, late, kept, sent):
    groups, rows, width = early.shape
    chunk = (groups, rows, width)
    slots = (groups - 1, rows, width)
    return pl.pallas_call(
        functools.partial(closing_kernel, groups),
        out_shape=(
            jax.ShapeDtypeStruct((rows, width), jnp.float32),
            jax.ShapeDtypeStruct((rows, width), jnp.float32),
            jax.ShapeDtypeStruct(kept.shape, jnp.float32),
        ),
        in_specs=[pl.BlockSpec(memory_space=pltpu.VMEM)] * 4,
        out_specs=[pl.BlockSpec(memory_space=pltpu.VMEM)] * 3,
        scratch_shapes=[
            pltpu.VMEM(chunk, jnp.bfloat16),
            pltpu.VMEM(slots, jnp.bfloat16),
            pltpu.VMEM((2,) + chunk, jnp.float32),
            pltpu.VMEM(chunk, jnp.bfloat16),
            pltpu.VMEM(chunk, jnp.bfloat16),
            pltpu.VMEM(chunk, jnp.float32),
            pltpu.VMEM(chunk, jnp.bfloat16),
            pltpu.VMEM(slots, jnp.bfloat16),
            pltpu.VMEM(kept.shape, jnp.float32),
            pltpu.SemaphoreType.DMA((3,)),
            pltpu.SemaphoreType.DMA((3,)),
            pltpu.SemaphoreType.DMA((groups - 1,)),
            pltpu.SemaphoreType.DMA((groups - 1,)),
            pltpu.SemaphoreType.DMA((groups - 1,)),
            pltpu.SemaphoreType.DMA((groups - 1,)),
        ],
        compiler_params=pltpu.CompilerParams(
            collective_id=0, has_side_effects=True, vmem_limit_bytes=48 * 1024 * 1024
        ),
    )(early, late, kept, sent)


def body(
    embedded, grad_out, mask_pos, timestep, time_table, mask_embed, w_query, w_key, w_value, w_out
):
    seq_index = lax.axis_index("seq")
    seq_count = lax.axis_size("seq")
    head_place = lax.axis_index("head")
    core, side = seq_index % 2, seq_index // 2 % 2
    slab_rows = embedded.shape[0]
    total_len = slab_rows * seq_count
    scale = HEAD_DIM ** (-0.5)
    full_rows = joined_heads(embedded, head_place)
    full_grad = joined_heads(grad_out, head_place)
    positions = seq_index * slab_rows + jnp.arange(slab_rows, dtype=jnp.int32)
    masked = jnp.any(positions[:, None] == mask_pos[None, :], axis=1)
    time_row = lax.dynamic_slice_in_dim(time_table, timestep[0], 1, 0).astype(jnp.float32)
    hidden = (
        jnp.where(
            masked[:, None], mask_embed.astype(jnp.float32)[None, :], full_rows.astype(jnp.float32)
        )
        + time_row
    ).astype(jnp.bfloat16)
    key_rows = jnp.dot(hidden, w_key, preferred_element_type=jnp.float32).astype(jnp.bfloat16)
    value_rows = jnp.dot(hidden, w_value, preferred_element_type=jnp.float32).astype(jnp.bfloat16)
    queries = jnp.dot(hidden, w_query, preferred_element_type=jnp.float32).astype(jnp.bfloat16)
    grad_attn = contract_last(full_grad, w_out).astype(jnp.bfloat16)
    group_width = queries.shape[1]
    head_count = group_width // HEAD_DIM

    own = jnp.concatenate([key_rows, value_rows], axis=1)
    below = passed_along(own, "seq", 4)
    above = passed_along(own, "seq", -4)
    plane_side = swapped(own, "seq", 2)
    plane_core = swapped(own, "seq", 1)
    far_side = swapped(jnp.where(side == 1, below, above), "seq", 2)
    far_core = swapped(jnp.where(core == 1, below, above), "seq", 1)
    plane_both = swapped(plane_side, "seq", 1)
    far_both = swapped(far_side, "seq", 1)
    slabs = jnp.concatenate(
        [far_both, plane_both, far_core, plane_core, far_side, plane_side, own, below, above],
        axis=0,
    )
    core_step = 4 - 8 * (1 - core)
    side_step = 4 - 8 * (1 - side)
    numbers = [
        (seq_index ^ 3) + side_step,
        seq_index ^ 3,
        (seq_index ^ 1) + core_step,
        seq_index ^ 1,
        (seq_index ^ 2) + side_step,
        seq_index ^ 2,
        seq_index,
        seq_index - 4,
        seq_index + 4,
    ]
    offsets = jnp.arange(slab_rows, dtype=jnp.int32)
    key_pos = jnp.concatenate([number * slab_rows + offsets for number in numbers])
    keys_all = slabs[:, :group_width]
    values_all = slabs[:, group_width:]
    distance_grid = positions[:, None] - key_pos[None, :]
    band = (
        (jnp.abs(distance_grid) <= HALF) & (key_pos[None, :] >= 0) & (key_pos[None, :] < total_len)
    )
    head_outputs = []
    query_grads = []
    key_grads = []
    value_grads = []
    for head_index in range(head_count):
        lower_col = head_index * HEAD_DIM
        upper_col = lower_col + HEAD_DIM
        head_query = queries[:, lower_col:upper_col]
        head_keys = keys_all[:, lower_col:upper_col]
        head_values = values_all[:, lower_col:upper_col]
        head_grad = grad_attn[:, lower_col:upper_col]
        scores = contract_last(head_query, head_keys) * scale
        scores = jnp.where(band, scores, NEG_FILL)
        row_max = jnp.max(scores, axis=1, keepdims=True)
        log_total = row_max + jnp.log(jnp.sum(jnp.exp(scores - row_max), axis=1, keepdims=True))
        attention = jnp.exp(scores - log_total)
        rounded = attention.astype(jnp.bfloat16)
        output = jnp.dot(rounded, head_values, preferred_element_type=jnp.float32).astype(
            jnp.bfloat16
        )
        head_outputs.append(output)
        delta = jnp.sum(head_grad.astype(jnp.float32) * output.astype(jnp.float32), axis=1)
        dprob = contract_last(head_grad, head_values)
        dscore = (attention * (dprob - delta[:, None])).astype(jnp.bfloat16)
        query_grads.append(scale * jnp.dot(dscore, head_keys, preferred_element_type=jnp.float32))
        key_grads.append(scale * contract_first(dscore, head_query))
        value_grads.append(contract_first(rounded, head_grad))
    attn_out = jnp.concatenate(head_outputs, axis=1)
    query_rounded = jnp.concatenate(query_grads, axis=1).astype(jnp.bfloat16)
    slab_grads = jnp.concatenate(key_grads + value_grads, axis=1)

    def slab_of(first, count):
        return slab_grads[first * slab_rows : (first + count) * slab_rows]

    by_core = swapped(slab_of(0, 4), "seq", 1)
    for_side = (by_core[: 2 * slab_rows] + slab_of(4, 2)).astype(jnp.bfloat16)
    early_part = core_summed(
        jnp.concatenate(
            [contract_first(hidden, query_rounded), contract_first(full_grad, attn_out)], axis=1
        ),
        seq_index,
    )
    by_side, early_part = lax.optimization_barrier((swapped(for_side, "seq", 2), early_part))
    by_side = by_side.astype(jnp.float32)
    early_part = side_summed(early_part, seq_index)
    core_far, core_own = by_core[2 * slab_rows : 3 * slab_rows], by_core[3 * slab_rows :]
    side_far, side_own = by_side[:slab_rows], by_side[slab_rows:]
    to_below = slab_of(7, 1) + jnp.where(core == 1, core_far, 0.0) + jnp.where(side == 1, side_far, 0.0)
    to_above = slab_of(8, 1) + jnp.where(core == 0, core_far, 0.0) + jnp.where(side == 0, side_far, 0.0)
    slab_total = slab_of(6, 1) + core_own + side_own
    slab_total = slab_total + passed_along(to_below.astype(jnp.bfloat16), "seq", -4).astype(jnp.float32)
    slab_total = slab_total + passed_along(to_above.astype(jnp.bfloat16), "seq", 4).astype(jnp.float32)
    pair_rounded = slab_total.astype(jnp.bfloat16)

    partial_grad = contract_last(query_rounded, w_query)
    partial_grad = partial_grad + contract_last(pair_rounded[:, :group_width], w_key)
    partial_grad = partial_grad + contract_last(pair_rounded[:, group_width:], w_value)
    half = embedded.shape[1]
    left, right = partial_grad[:, :half], partial_grad[:, half:]
    kept = jnp.where(head_place == 0, left, right)
    sent = jnp.where(head_place == 0, right, left)
    late_part = contract_first(hidden, pair_rounded)
    groups = seq_count // 4
    if groups > 4:
        early = group_summed(early_part)
        late = group_summed(side_summed(core_summed(late_part, seq_index), seq_index))
        summed = kept + swapped(sent, "head", 1)
    else:
        rows = late_part.shape[0] // seq_count
        blocks = late_part.reshape(groups, 2, 2, rows, late_part.shape[1]).transpose(2, 1, 0, 3, 4)
        early, late, summed = closing_sums(early_part, blocks, kept, sent)
    input_grad = jnp.where(masked[:, None], 0.0, summed).astype(jnp.bfloat16)
    return (
        input_grad,
        early[:, :group_width],
        late[:, :group_width],
        late[:, group_width:],
        early[:, group_width:],
    )


def solution(mesh):
    placed = (
        P("seq", "head"),
        P("seq", "head"),
        P("seq"),
        P(),
        P(),
        P(),
        P(None, "head"),
        P(None, "head"),
        P(None, "head"),
        P("head", None),
    )
    return jax.shard_map(
        body,
        mesh=mesh,
        in_specs=placed,
        out_specs=(
            P("seq", "head"),
            P("seq", "head"),
            P("seq", "head"),
            P("seq", "head"),
            P("seq", "head"),
        ),
        check_vma=False,
    )
```

```python
import functools

import jax
import jax.numpy as jnp
from jax import lax
from jax.experimental import pallas as pl
from jax.experimental.pallas import tpu as pltpu
from jax.sharding import PartitionSpec as P

HEAD_DIM = 64
HALF = 1024


NEG_FILL = -1e30


def contract_first(left, right):
    return lax.dot_general(
        left, right, (((0,), (0,)), ((), ())), preferred_element_type=jnp.float32
    )


def contract_last(left, right):
    return lax.dot_general(
        left, right, (((1,), (1,)), ((), ())), preferred_element_type=jnp.float32
    )


def contract_mixed(left, right):
    return lax.dot_general(
        left, right, (((0,), (1,)), ((), ())), preferred_element_type=jnp.float32
    )


def swapped(value, axis, bit):
    count = lax.axis_size(axis)
    return lax.ppermute(value, axis, [(source, source ^ bit) for source in range(count)])


def passed_along(value, axis, steps):
    count = lax.axis_size(axis)
    first, last = (max(0, -steps), min(count, count - steps))
    return lax.ppermute(value, axis, [(source, source + steps) for source in range(first, last)])


def picked(array, index, axis):
    return lax.dynamic_index_in_dim(array, index, axis, keepdims=False)


def joined_heads(mine, head_index):
    other = swapped(mine, "head", 1)
    first = jnp.where(head_index == 0, mine, other)
    second = jnp.where(head_index == 0, other, mine)
    return jnp.concatenate([first, second], axis=1)


def core_summed(parts, seq_index):
    count = lax.axis_size("seq")
    core = seq_index % 2
    blocks = [part.reshape(count // 4, 2, 2, -1, part.shape[1]) for part in parts]
    kept = jnp.concatenate([picked(block, core, 2) for block in blocks], axis=3)
    sent = jnp.concatenate([picked(block, 1 - core, 2) for block in blocks], axis=3)
    return kept + swapped(sent, "seq", 1)


def side_summed(blocks, seq_index):
    side = seq_index // 2 % 2
    sent = picked(blocks, 1 - side, 1).astype(jnp.bfloat16)
    return picked(blocks, side, 1) + swapped(sent, "seq", 2).astype(jnp.float32)


def group_summed(blocks):
    groups, rows, width = blocks.shape
    members = [[g * 4 + place for g in range(groups)] for place in range(4)]
    return lax.psum_scatter(
        blocks.reshape(groups * rows, width),
        "seq",
        scatter_dimension=0,
        axis_index_groups=members,
        tiled=True,
    )


def closing_kernel(
    groups,
    early_ref,
    late_ref,
    kept_ref,
    sent_ref,
    early_out,
    late_out,
    summed_out,
    early_send,
    early_slots,
    core_slot,
    side_send,
    side_slot,
    total,
    late_send,
    late_slots,
    head_slot,
    single_send,
    single_recv,
    early_send_sems,
    early_recv_sems,
    late_send_sems,
    late_recv_sems,
):
    me = lax.axis_index("seq")
    head = lax.axis_index("head")
    core = lax.rem(me, 2)
    side = lax.rem(me // 2, 2)
    group = me // 4
    place = lax.rem(me, 4)
    core_peer = me + 1 - 2 * core
    side_peer = me + 2 - 4 * side
    targets = [lax.rem(group + step, groups) for step in range(1, groups)]
    peers = [(core_peer, head), (side_peer, head), (me, 1 - head)]
    peers += [(target * 4 + place, head) for target in targets]

    barrier = pltpu.get_barrier_semaphore()
    for peer in peers:
        pl.semaphore_signal(barrier, inc=1, device_id=peer, device_id_type=pl.DeviceIdType.MESH)
    pl.semaphore_wait(barrier, len(peers))

    def remote(source, target, send, recv, peer):
        copy = pltpu.make_async_remote_copy(
            src_ref=source,
            dst_ref=target,
            send_sem=send,
            recv_sem=recv,
            device_id=peer,
            device_id_type=pl.DeviceIdType.MESH,
        )
        copy.start()
        return copy

    core_copy = remote(
        late_ref.at[1 - core], core_slot, single_send.at[0], single_recv.at[0], peers[0]
    )
    early_send[...] = early_ref[...].astype(jnp.bfloat16)
    early_copies = []
    for step in range(1, groups):
        early_copies.append(
            remote(
                early_send.at[targets[step - 1]],
                early_slots.at[step - 1],
                early_send_sems.at[step - 1],
                early_recv_sems.at[step - 1],
                peers[2 + step],
            )
        )
    head_copy = remote(sent_ref, head_slot, single_send.at[2], single_recv.at[2], peers[2])
    core_copy.wait()
    side_send[...] = (late_ref[core, 1 - side] + core_slot[1 - side]).astype(jnp.bfloat16)
    side_copy = remote(side_send, side_slot, single_send.at[1], single_recv.at[1], peers[1])
    total[...] = late_ref[core, side] + core_slot[side]
    side_copy.wait()
    total[...] = total[...] + side_slot[...].astype(jnp.float32)
    late_send[...] = total[...].astype(jnp.bfloat16)
    late_copies = []
    for step in range(1, groups):
        late_copies.append(
            remote(
                late_send.at[targets[step - 1]],
                late_slots.at[step - 1],
                late_send_sems.at[step - 1],
                late_recv_sems.at[step - 1],
                peers[2 + step],
            )
        )
    head_copy.wait()
    summed_out[...] = kept_ref[...] + head_slot[...]
    result = early_ref[group]
    for step in range(1, groups):
        early_copies[step - 1].wait()
        result = result + early_slots[step - 1].astype(jnp.float32)
    early_out[...] = result
    result = total[group]
    for step in range(1, groups):
        late_copies[step - 1].wait()
        result = result + late_slots[step - 1].astype(jnp.float32)
    late_out[...] = result


def closing_sums(early, late, kept, sent):
    groups, rows, width = early.shape
    chunk = (groups, rows, width)
    slots = (groups - 1, rows, width)
    return pl.pallas_call(
        functools.partial(closing_kernel, groups),
        out_shape=(
            jax.ShapeDtypeStruct((rows, width), jnp.float32),
            jax.ShapeDtypeStruct((rows, width), jnp.float32),
            jax.ShapeDtypeStruct(kept.shape, jnp.float32),
        ),
        in_specs=[pl.BlockSpec(memory_space=pltpu.VMEM)] * 4,
        out_specs=[pl.BlockSpec(memory_space=pltpu.VMEM)] * 3,
        scratch_shapes=[
            pltpu.VMEM(chunk, jnp.bfloat16),
            pltpu.VMEM(slots, jnp.bfloat16),
            pltpu.VMEM((2,) + chunk, jnp.float32),
            pltpu.VMEM(chunk, jnp.bfloat16),
            pltpu.VMEM(chunk, jnp.bfloat16),
            pltpu.VMEM(chunk, jnp.float32),
            pltpu.VMEM(chunk, jnp.bfloat16),
            pltpu.VMEM(slots, jnp.bfloat16),
            pltpu.VMEM(kept.shape, jnp.float32),
            pltpu.SemaphoreType.DMA((3,)),
            pltpu.SemaphoreType.DMA((3,)),
            pltpu.SemaphoreType.DMA((groups - 1,)),
            pltpu.SemaphoreType.DMA((groups - 1,)),
            pltpu.SemaphoreType.DMA((groups - 1,)),
            pltpu.SemaphoreType.DMA((groups - 1,)),
        ],
        compiler_params=pltpu.CompilerParams(
            collective_id=0, has_side_effects=True, vmem_limit_bytes=48 * 1024 * 1024
        ),
    )(early, late, kept, sent)


def body(
    embedded, grad_out, mask_pos, timestep, time_table, mask_embed, w_query, w_key, w_value, w_out
):
    seq_index = lax.axis_index("seq")
    seq_count = lax.axis_size("seq")
    head_place = lax.axis_index("head")
    core, side = seq_index % 2, seq_index // 2 % 2
    slab_rows = embedded.shape[0]
    total_len = slab_rows * seq_count
    scale = HEAD_DIM ** (-0.5)
    full_rows = joined_heads(embedded, head_place)
    full_grad = joined_heads(grad_out, head_place)
    positions = seq_index * slab_rows + jnp.arange(slab_rows, dtype=jnp.int32)
    masked = jnp.any(positions[:, None] == mask_pos[None, :], axis=1)
    time_row = lax.dynamic_slice_in_dim(time_table, timestep[0], 1, 0).astype(jnp.float32)
    hidden = (
        jnp.where(
            masked[:, None], mask_embed.astype(jnp.float32)[None, :], full_rows.astype(jnp.float32)
        )
        + time_row
    ).astype(jnp.bfloat16)
    key_rows = jnp.dot(hidden, w_key, preferred_element_type=jnp.float32).astype(jnp.bfloat16)
    value_rows = jnp.dot(hidden, w_value, preferred_element_type=jnp.float32).astype(jnp.bfloat16)
    queries = jnp.dot(hidden, w_query, preferred_element_type=jnp.float32).astype(jnp.bfloat16)
    grad_attn = contract_last(full_grad, w_out).astype(jnp.bfloat16)
    group_width = queries.shape[1]
    head_count = group_width // HEAD_DIM

    own = jnp.concatenate([key_rows, value_rows], axis=1)
    below = passed_along(own, "seq", 4)
    above = passed_along(own, "seq", -4)
    plane_side = swapped(own, "seq", 2)
    plane_core = swapped(own, "seq", 1)
    far_side = swapped(jnp.where(side == 1, below, above), "seq", 2)
    far_core = swapped(jnp.where(core == 1, below, above), "seq", 1)
    plane_both = swapped(plane_side, "seq", 1)
    far_both = swapped(far_side, "seq", 1)
    slabs = jnp.concatenate(
        [far_both, plane_both, far_core, plane_core, far_side, plane_side, own, below, above],
        axis=0,
    )
    core_step = 4 - 8 * (1 - core)
    side_step = 4 - 8 * (1 - side)
    numbers = [
        (seq_index ^ 3) + side_step,
        seq_index ^ 3,
        (seq_index ^ 1) + core_step,
        seq_index ^ 1,
        (seq_index ^ 2) + side_step,
        seq_index ^ 2,
        seq_index,
        seq_index - 4,
        seq_index + 4,
    ]
    offsets = jnp.arange(slab_rows, dtype=jnp.int32)
    key_pos = jnp.concatenate([number * slab_rows + offsets for number in numbers])
    keys_all = slabs[:, :group_width]
    values_all = slabs[:, group_width:]
    distance_grid = positions[:, None] - key_pos[None, :]
    band = (
        (jnp.abs(distance_grid) <= HALF) & (key_pos[None, :] >= 0) & (key_pos[None, :] < total_len)
    )
    head_outputs = []
    query_grads = []
    key_grads = []
    value_grads = []
    for head_index in range(head_count):
        lower_col = head_index * HEAD_DIM
        upper_col = lower_col + HEAD_DIM
        head_query = queries[:, lower_col:upper_col]
        head_keys = keys_all[:, lower_col:upper_col]
        head_values = values_all[:, lower_col:upper_col]
        head_grad = grad_attn[:, lower_col:upper_col]
        scores = contract_last(head_query, head_keys) * scale
        scores = jnp.where(band, scores, NEG_FILL)
        row_max = jnp.max(scores, axis=1, keepdims=True)
        log_total = row_max + jnp.log(jnp.sum(jnp.exp(scores - row_max), axis=1, keepdims=True))
        attention = jnp.exp(scores - log_total)
        rounded = attention.astype(jnp.bfloat16)
        output = jnp.dot(rounded, head_values, preferred_element_type=jnp.float32).astype(
            jnp.bfloat16
        )
        head_outputs.append(output)
        delta = jnp.sum(head_grad.astype(jnp.float32) * output.astype(jnp.float32), axis=1)
        dprob = contract_last(head_grad, head_values)
        dscore = (attention * (dprob - delta[:, None])).astype(jnp.bfloat16)
        query_grads.append(scale * jnp.dot(dscore, head_keys, preferred_element_type=jnp.float32))
        key_grads.append(scale * contract_first(head_query, dscore))
        value_grads.append(contract_first(head_grad, rounded))
    attn_out = jnp.concatenate(head_outputs, axis=1)
    query_rounded = jnp.concatenate(query_grads, axis=1).astype(jnp.bfloat16)
    slab_grads = jnp.concatenate(key_grads + value_grads, axis=0)

    def slab_of(first, count):
        return slab_grads[:, first * slab_rows : (first + count) * slab_rows]

    by_core = swapped(slab_of(0, 4), "seq", 1)
    for_side = (by_core[:, : 2 * slab_rows] + slab_of(4, 2)).astype(jnp.bfloat16)
    early_part = core_summed(
        [contract_first(hidden, query_rounded), contract_first(full_grad, attn_out)], seq_index
    )
    by_side, early_part = lax.optimization_barrier((swapped(for_side, "seq", 2), early_part))
    by_side = by_side.astype(jnp.float32)
    early_part = side_summed(early_part, seq_index)
    core_far, core_own = by_core[:, 2 * slab_rows : 3 * slab_rows], by_core[:, 3 * slab_rows :]
    side_far, side_own = by_side[:, :slab_rows], by_side[:, slab_rows:]
    to_below = slab_of(7, 1) + jnp.where(core == 1, core_far, 0.0) + jnp.where(side == 1, side_far, 0.0)
    to_above = slab_of(8, 1) + jnp.where(core == 0, core_far, 0.0) + jnp.where(side == 0, side_far, 0.0)
    slab_total = slab_of(6, 1) + core_own + side_own
    slab_total = slab_total + passed_along(to_below.astype(jnp.bfloat16), "seq", -4).astype(jnp.float32)
    slab_total = slab_total + passed_along(to_above.astype(jnp.bfloat16), "seq", 4).astype(jnp.float32)
    pair_rounded = slab_total.astype(jnp.bfloat16)

    partial_grad = contract_last(query_rounded, w_query)
    partial_grad = partial_grad + contract_mixed(pair_rounded[:group_width], w_key)
    partial_grad = partial_grad + contract_mixed(pair_rounded[group_width:], w_value)
    half = embedded.shape[1]
    left, right = partial_grad[:, :half], partial_grad[:, half:]
    kept = jnp.where(head_place == 0, left, right)
    sent = jnp.where(head_place == 0, right, left)
    late_part = lax.dot_general(
        hidden, pair_rounded, (((0,), (1,)), ((), ())), preferred_element_type=jnp.float32
    )
    groups = seq_count // 4
    if groups > 4:
        early = group_summed(early_part)
        late = group_summed(side_summed(core_summed([late_part], seq_index), seq_index))
        summed = kept + swapped(sent, "head", 1)
    else:
        rows = late_part.shape[0] // seq_count
        blocks = late_part.reshape(groups, 2, 2, rows, late_part.shape[1]).transpose(2, 1, 0, 3, 4)
        early, late, summed = closing_sums(early_part, blocks, kept, sent)
    input_grad = jnp.where(masked[:, None], 0.0, summed).astype(jnp.bfloat16)
    return (
        input_grad,
        early[:, :group_width],
        late[:, :group_width],
        late[:, group_width:],
        early[:, group_width:],
    )


def solution(mesh):
    placed = (
        P("seq", "head"),
        P("seq", "head"),
        P("seq"),
        P(),
        P(),
        P(),
        P(None, "head"),
        P(None, "head"),
        P(None, "head"),
        P("head", None),
    )
    return jax.shard_map(
        body,
        mesh=mesh,
        in_specs=placed,
        out_specs=(
            P("seq", "head"),
            P("seq", "head"),
            P("seq", "head"),
            P("seq", "head"),
            P("seq", "head"),
        ),
        check_vma=False,
    )
```

```python
import functools

import jax
import jax.numpy as jnp
from jax import lax
from jax.experimental import pallas as pl
from jax.experimental.pallas import tpu as pltpu
from jax.sharding import PartitionSpec as P

HEAD_DIM = 64
HALF = 1024


NEG_FILL = -1e30


def contract_first(left, right):
    return lax.dot_general(
        left, right, (((0,), (0,)), ((), ())), preferred_element_type=jnp.float32
    )


def contract_last(left, right):
    return lax.dot_general(
        left, right, (((1,), (1,)), ((), ())), preferred_element_type=jnp.float32
    )


def contract_mixed(left, right):
    return lax.dot_general(
        left, right, (((0,), (1,)), ((), ())), preferred_element_type=jnp.float32
    )


def swapped(value, axis, bit):
    count = lax.axis_size(axis)
    return lax.ppermute(value, axis, [(source, source ^ bit) for source in range(count)])


def passed_along(value, axis, steps):
    count = lax.axis_size(axis)
    first, last = (max(0, -steps), min(count, count - steps))
    return lax.ppermute(value, axis, [(source, source + steps) for source in range(first, last)])


def picked(array, index, axis):
    return lax.dynamic_index_in_dim(array, index, axis, keepdims=False)


def joined_heads(mine, head_index):
    other = swapped(mine, "head", 1)
    first = jnp.where(head_index == 0, mine, other)
    second = jnp.where(head_index == 0, other, mine)
    return jnp.concatenate([first, second], axis=1)


def core_summed(parts, seq_index):
    count = lax.axis_size("seq")
    core = seq_index % 2
    blocks = [part.reshape(count // 4, 2, 2, -1, part.shape[1]) for part in parts]
    kept = jnp.concatenate([picked(block, core, 2) for block in blocks], axis=3)
    sent = jnp.concatenate([picked(block, 1 - core, 2) for block in blocks], axis=3)
    return kept + swapped(sent, "seq", 1)


def side_summed(blocks, seq_index):
    side = seq_index // 2 % 2
    sent = picked(blocks, 1 - side, 1).astype(jnp.bfloat16)
    return picked(blocks, side, 1) + swapped(sent, "seq", 2).astype(jnp.float32)


def group_summed(blocks):
    groups, rows, width = blocks.shape
    members = [[g * 4 + place for g in range(groups)] for place in range(4)]
    return lax.psum_scatter(
        blocks.reshape(groups * rows, width),
        "seq",
        scatter_dimension=0,
        axis_index_groups=members,
        tiled=True,
    )


def closing_kernel(
    groups,
    early_ref,
    late_ref,
    kept_ref,
    sent_ref,
    early_out,
    late_out,
    summed_out,
    early_send,
    early_slots,
    core_slot,
    side_send,
    side_slot,
    total,
    late_send,
    late_slots,
    head_slot,
    single_send,
    single_recv,
    early_send_sems,
    early_recv_sems,
    late_send_sems,
    late_recv_sems,
    core_send_sems,
    core_recv_sems,
    side_send_sems,
    side_recv_sems,
):
    me = lax.axis_index("seq")
    head = lax.axis_index("head")
    core = lax.rem(me, 2)
    side = lax.rem(me // 2, 2)
    group = me // 4
    place = lax.rem(me, 4)
    core_peer = me + 1 - 2 * core
    side_peer = me + 2 - 4 * side
    targets = [lax.rem(group + step, groups) for step in range(1, groups)]
    peers = [(core_peer, head), (side_peer, head), (me, 1 - head)]
    peers += [(target * 4 + place, head) for target in targets]

    barrier = pltpu.get_barrier_semaphore()
    for peer in peers:
        pl.semaphore_signal(barrier, inc=1, device_id=peer, device_id_type=pl.DeviceIdType.MESH)
    pl.semaphore_wait(barrier, len(peers))

    def remote(source, target, send, recv, peer):
        copy = pltpu.make_async_remote_copy(
            src_ref=source,
            dst_ref=target,
            send_sem=send,
            recv_sem=recv,
            device_id=peer,
            device_id_type=pl.DeviceIdType.MESH,
        )
        copy.start()
        return copy

    order = targets + [group]
    core_copies = []
    for piece, owner in enumerate(order):
        core_copies.append(
            remote(
                late_ref.at[1 - core, owner],
                core_slot.at[piece],
                core_send_sems.at[piece],
                core_recv_sems.at[piece],
                peers[0],
            )
        )
    early_send[...] = early_ref[...].astype(jnp.bfloat16)
    early_copies = []
    for step in range(1, groups):
        early_copies.append(
            remote(
                early_send.at[targets[step - 1]],
                early_slots.at[step - 1],
                early_send_sems.at[step - 1],
                early_recv_sems.at[step - 1],
                peers[2 + step],
            )
        )
    head_copy = remote(sent_ref, head_slot, single_send.at[0], single_recv.at[0], peers[2])
    side_copies = []
    for piece, owner in enumerate(order):
        core_copies[piece].wait()
        side_send[piece] = (
            late_ref[core, owner, 1 - side] + core_slot[piece, 1 - side]
        ).astype(jnp.bfloat16)
        side_copies.append(
            remote(
                side_send.at[piece],
                side_slot.at[piece],
                side_send_sems.at[piece],
                side_recv_sems.at[piece],
                peers[1],
            )
        )
        total[piece] = late_ref[core, owner, side] + core_slot[piece, side]
    late_copies = []
    for piece in range(groups):
        side_copies[piece].wait()
        total[piece] = total[piece] + side_slot[piece].astype(jnp.float32)
        if piece < groups - 1:
            late_send[piece] = total[piece].astype(jnp.bfloat16)
            late_copies.append(
                remote(
                    late_send.at[piece],
                    late_slots.at[piece],
                    late_send_sems.at[piece],
                    late_recv_sems.at[piece],
                    peers[3 + piece],
                )
            )
    head_copy.wait()
    summed_out[...] = kept_ref[...] + head_slot[...]
    result = early_ref[group]
    for step in range(1, groups):
        early_copies[step - 1].wait()
        result = result + early_slots[step - 1].astype(jnp.float32)
    early_out[...] = result
    result = total[groups - 1]
    for step in range(1, groups):
        late_copies[step - 1].wait()
        result = result + late_slots[step - 1].astype(jnp.float32)
    late_out[...] = result


def closing_sums(early, late, kept, sent):
    groups, rows, width = early.shape
    chunk = (groups, rows, width)
    slots = (groups - 1, rows, width)
    return pl.pallas_call(
        functools.partial(closing_kernel, groups),
        out_shape=(
            jax.ShapeDtypeStruct((rows, width), jnp.float32),
            jax.ShapeDtypeStruct((rows, width), jnp.float32),
            jax.ShapeDtypeStruct(kept.shape, jnp.float32),
        ),
        in_specs=[pl.BlockSpec(memory_space=pltpu.VMEM)] * 4,
        out_specs=[pl.BlockSpec(memory_space=pltpu.VMEM)] * 3,
        scratch_shapes=[
            pltpu.VMEM(chunk, jnp.bfloat16),
            pltpu.VMEM(slots, jnp.bfloat16),
            pltpu.VMEM((groups, 2, rows, width), jnp.float32),
            pltpu.VMEM(chunk, jnp.bfloat16),
            pltpu.VMEM(chunk, jnp.bfloat16),
            pltpu.VMEM(chunk, jnp.float32),
            pltpu.VMEM(chunk, jnp.bfloat16),
            pltpu.VMEM(slots, jnp.bfloat16),
            pltpu.VMEM(kept.shape, jnp.float32),
            pltpu.SemaphoreType.DMA((1,)),
            pltpu.SemaphoreType.DMA((1,)),
            pltpu.SemaphoreType.DMA((groups - 1,)),
            pltpu.SemaphoreType.DMA((groups - 1,)),
            pltpu.SemaphoreType.DMA((groups - 1,)),
            pltpu.SemaphoreType.DMA((groups - 1,)),
            pltpu.SemaphoreType.DMA((groups,)),
            pltpu.SemaphoreType.DMA((groups,)),
            pltpu.SemaphoreType.DMA((groups,)),
            pltpu.SemaphoreType.DMA((groups,)),
        ],
        compiler_params=pltpu.CompilerParams(
            collective_id=0, has_side_effects=True, vmem_limit_bytes=48 * 1024 * 1024
        ),
    )(early, late, kept, sent)


def body(
    embedded, grad_out, mask_pos, timestep, time_table, mask_embed, w_query, w_key, w_value, w_out
):
    seq_index = lax.axis_index("seq")
    seq_count = lax.axis_size("seq")
    head_place = lax.axis_index("head")
    core, side = seq_index % 2, seq_index // 2 % 2
    slab_rows = embedded.shape[0]
    total_len = slab_rows * seq_count
    scale = HEAD_DIM ** (-0.5)
    full_rows = joined_heads(embedded, head_place)
    full_grad = joined_heads(grad_out, head_place)
    positions = seq_index * slab_rows + jnp.arange(slab_rows, dtype=jnp.int32)
    masked = jnp.any(positions[:, None] == mask_pos[None, :], axis=1)
    time_row = lax.dynamic_slice_in_dim(time_table, timestep[0], 1, 0).astype(jnp.float32)
    hidden = (
        jnp.where(
            masked[:, None], mask_embed.astype(jnp.float32)[None, :], full_rows.astype(jnp.float32)
        )
        + time_row
    ).astype(jnp.bfloat16)
    key_rows = jnp.dot(hidden, w_key, preferred_element_type=jnp.float32).astype(jnp.bfloat16)
    value_rows = jnp.dot(hidden, w_value, preferred_element_type=jnp.float32).astype(jnp.bfloat16)
    queries = jnp.dot(hidden, w_query, preferred_element_type=jnp.float32).astype(jnp.bfloat16)
    grad_attn = contract_last(full_grad, w_out).astype(jnp.bfloat16)
    group_width = queries.shape[1]
    head_count = group_width // HEAD_DIM

    own = jnp.concatenate([key_rows, value_rows], axis=1)
    below = passed_along(own, "seq", 4)
    above = passed_along(own, "seq", -4)
    plane_side = swapped(own, "seq", 2)
    plane_core = swapped(own, "seq", 1)
    far_side = swapped(jnp.where(side == 1, below, above), "seq", 2)
    far_core = swapped(jnp.where(core == 1, below, above), "seq", 1)
    plane_both = swapped(plane_side, "seq", 1)
    far_both = swapped(far_side, "seq", 1)
    slabs = jnp.concatenate(
        [far_both, plane_both, far_core, plane_core, far_side, plane_side, own, below, above],
        axis=0,
    )
    core_step = 4 - 8 * (1 - core)
    side_step = 4 - 8 * (1 - side)
    numbers = [
        (seq_index ^ 3) + side_step,
        seq_index ^ 3,
        (seq_index ^ 1) + core_step,
        seq_index ^ 1,
        (seq_index ^ 2) + side_step,
        seq_index ^ 2,
        seq_index,
        seq_index - 4,
        seq_index + 4,
    ]
    offsets = jnp.arange(slab_rows, dtype=jnp.int32)
    key_pos = jnp.concatenate([number * slab_rows + offsets for number in numbers])
    keys_all = slabs[:, :group_width]
    values_all = slabs[:, group_width:]
    distance_grid = positions[:, None] - key_pos[None, :]
    band = (
        (jnp.abs(distance_grid) <= HALF) & (key_pos[None, :] >= 0) & (key_pos[None, :] < total_len)
    )
    head_outputs = []
    query_grads = []
    key_grads = []
    value_grads = []
    for head_index in range(head_count):
        lower_col = head_index * HEAD_DIM
        upper_col = lower_col + HEAD_DIM
        head_query = queries[:, lower_col:upper_col]
        head_keys = keys_all[:, lower_col:upper_col]
        head_values = values_all[:, lower_col:upper_col]
        head_grad = grad_attn[:, lower_col:upper_col]
        scores = contract_last(head_query, head_keys) * scale
        scores = jnp.where(band, scores, NEG_FILL)
        row_max = jnp.max(scores, axis=1, keepdims=True)
        log_total = row_max + jnp.log(jnp.sum(jnp.exp(scores - row_max), axis=1, keepdims=True))
        attention = jnp.exp(scores - log_total)
        rounded = attention.astype(jnp.bfloat16)
        output = jnp.dot(rounded, head_values, preferred_element_type=jnp.float32).astype(
            jnp.bfloat16
        )
        head_outputs.append(output)
        delta = jnp.sum(head_grad.astype(jnp.float32) * output.astype(jnp.float32), axis=1)
        dprob = contract_last(head_grad, head_values)
        dscore = (attention * (dprob - delta[:, None])).astype(jnp.bfloat16)
        query_grads.append(scale * jnp.dot(dscore, head_keys, preferred_element_type=jnp.float32))
        key_grads.append(scale * contract_first(head_query, dscore))
        value_grads.append(contract_first(head_grad, rounded))
    attn_out = jnp.concatenate(head_outputs, axis=1)
    query_rounded = jnp.concatenate(query_grads, axis=1).astype(jnp.bfloat16)
    slab_grads = jnp.concatenate(key_grads + value_grads, axis=0)

    def slab_of(first, count):
        return slab_grads[:, first * slab_rows : (first + count) * slab_rows]

    by_core = swapped(slab_of(0, 4), "seq", 1)
    for_side = (by_core[:, : 2 * slab_rows] + slab_of(4, 2)).astype(jnp.bfloat16)
    early_part = core_summed(
        [contract_first(hidden, query_rounded), contract_first(full_grad, attn_out)], seq_index
    )
    by_side, early_part = lax.optimization_barrier((swapped(for_side, "seq", 2), early_part))
    by_side = by_side.astype(jnp.float32)
    early_part = side_summed(early_part, seq_index)
    core_far, core_own = by_core[:, 2 * slab_rows : 3 * slab_rows], by_core[:, 3 * slab_rows :]
    side_far, side_own = by_side[:, :slab_rows], by_side[:, slab_rows:]
    to_below = slab_of(7, 1) + jnp.where(core == 1, core_far, 0.0) + jnp.where(side == 1, side_far, 0.0)
    to_above = slab_of(8, 1) + jnp.where(core == 0, core_far, 0.0) + jnp.where(side == 0, side_far, 0.0)
    slab_total = slab_of(6, 1) + core_own + side_own
    slab_total = slab_total + passed_along(to_below.astype(jnp.bfloat16), "seq", -4).astype(jnp.float32)
    slab_total = slab_total + passed_along(to_above.astype(jnp.bfloat16), "seq", 4).astype(jnp.float32)
    pair_rounded = slab_total.astype(jnp.bfloat16)

    partial_grad = contract_last(query_rounded, w_query)
    partial_grad = partial_grad + contract_mixed(pair_rounded[:group_width], w_key)
    partial_grad = partial_grad + contract_mixed(pair_rounded[group_width:], w_value)
    half = embedded.shape[1]
    left, right = partial_grad[:, :half], partial_grad[:, half:]
    kept = jnp.where(head_place == 0, left, right)
    sent = jnp.where(head_place == 0, right, left)
    late_part = lax.dot_general(
        hidden, pair_rounded, (((0,), (1,)), ((), ())), preferred_element_type=jnp.float32
    )
    groups = seq_count // 4
    if groups > 4:
        early = group_summed(early_part)
        late = group_summed(side_summed(core_summed([late_part], seq_index), seq_index))
        summed = kept + swapped(sent, "head", 1)
    else:
        rows = late_part.shape[0] // seq_count
        blocks = late_part.reshape(groups, 2, 2, rows, late_part.shape[1]).transpose(2, 0, 1, 3, 4)
        early, late, summed = closing_sums(early_part, blocks, kept, sent)
    input_grad = jnp.where(masked[:, None], 0.0, summed).astype(jnp.bfloat16)
    return (
        input_grad,
        early[:, :group_width],
        late[:, :group_width],
        late[:, group_width:],
        early[:, group_width:],
    )


def solution(mesh):
    placed = (
        P("seq", "head"),
        P("seq", "head"),
        P("seq"),
        P(),
        P(),
        P(),
        P(None, "head"),
        P(None, "head"),
        P(None, "head"),
        P("head", None),
    )
    return jax.shard_map(
        body,
        mesh=mesh,
        in_specs=placed,
        out_specs=(
            P("seq", "head"),
            P("seq", "head"),
            P("seq", "head"),
            P("seq", "head"),
            P("seq", "head"),
        ),
        check_vma=False,
    )
```

```python
import functools

import jax
import jax.numpy as jnp
from jax import lax
from jax.experimental import pallas as pl
from jax.experimental.pallas import tpu as pltpu
from jax.sharding import PartitionSpec as P

HEAD_DIM = 64
HALF = 1024


NEG_FILL = -1e30


def contract_first(left, right):
    return lax.dot_general(
        left, right, (((0,), (0,)), ((), ())), preferred_element_type=jnp.float32
    )


def contract_last(left, right):
    return lax.dot_general(
        left, right, (((1,), (1,)), ((), ())), preferred_element_type=jnp.float32
    )


def contract_mixed(left, right):
    return lax.dot_general(
        left, right, (((0,), (1,)), ((), ())), preferred_element_type=jnp.float32
    )


def swapped(value, axis, bit):
    count = lax.axis_size(axis)
    return lax.ppermute(value, axis, [(source, source ^ bit) for source in range(count)])


def passed_along(value, axis, steps):
    count = lax.axis_size(axis)
    first, last = (max(0, -steps), min(count, count - steps))
    return lax.ppermute(value, axis, [(source, source + steps) for source in range(first, last)])


def picked(array, index, axis):
    return lax.dynamic_index_in_dim(array, index, axis, keepdims=False)


def joined_heads(mine, head_index):
    other = swapped(mine, "head", 1)
    first = jnp.where(head_index == 0, mine, other)
    second = jnp.where(head_index == 0, other, mine)
    return jnp.concatenate([first, second], axis=1)


def core_summed(parts, seq_index):
    count = lax.axis_size("seq")
    core = seq_index % 2
    blocks = [part.reshape(count // 4, 2, 2, -1, part.shape[1]) for part in parts]
    kept = jnp.concatenate([picked(block, core, 2) for block in blocks], axis=3)
    sent = jnp.concatenate([picked(block, 1 - core, 2) for block in blocks], axis=3)
    return kept + swapped(sent, "seq", 1)


def side_summed(blocks, seq_index):
    side = seq_index // 2 % 2
    sent = picked(blocks, 1 - side, 1).astype(jnp.bfloat16)
    return picked(blocks, side, 1) + swapped(sent, "seq", 2).astype(jnp.float32)


def group_summed(blocks):
    groups, rows, width = blocks.shape
    members = [[g * 4 + place for g in range(groups)] for place in range(4)]
    return lax.psum_scatter(
        blocks.reshape(groups * rows, width),
        "seq",
        scatter_dimension=0,
        axis_index_groups=members,
        tiled=True,
    )


def closing_kernel(
    groups,
    early_ref,
    late_ref,
    kept_ref,
    sent_ref,
    early_out,
    late_out,
    summed_out,
    early_send,
    early_slots,
    core_slot,
    side_send,
    side_slot,
    total,
    late_send,
    late_slots,
    head_slot,
    single_send,
    single_recv,
    early_send_sems,
    early_recv_sems,
    late_send_sems,
    late_recv_sems,
    core_send_sems,
    core_recv_sems,
    side_send_sems,
    side_recv_sems,
):
    me = lax.axis_index("seq")
    head = lax.axis_index("head")
    core = lax.rem(me, 2)
    side = lax.rem(me // 2, 2)
    group = me // 4
    place = lax.rem(me, 4)
    core_peer = me + 1 - 2 * core
    side_peer = me + 2 - 4 * side
    targets = [lax.rem(group + step, groups) for step in range(1, groups)]
    peers = [(core_peer, head), (side_peer, head), (me, 1 - head)]
    peers += [(target * 4 + place, head) for target in targets]

    barrier = pltpu.get_barrier_semaphore()
    for peer in peers:
        pl.semaphore_signal(barrier, inc=1, device_id=peer, device_id_type=pl.DeviceIdType.MESH)
    pl.semaphore_wait(barrier, len(peers))

    def remote(source, target, send, recv, peer):
        copy = pltpu.make_async_remote_copy(
            src_ref=source,
            dst_ref=target,
            send_sem=send,
            recv_sem=recv,
            device_id=peer,
            device_id_type=pl.DeviceIdType.MESH,
        )
        copy.start()
        return copy

    order = targets + [group]
    core_copies = []
    for piece, owner in enumerate(order):
        core_copies.append(
            remote(
                late_ref.at[1 - core, owner],
                core_slot.at[piece],
                core_send_sems.at[piece],
                core_recv_sems.at[piece],
                peers[0],
            )
        )
    early_send[...] = early_ref[...].astype(jnp.bfloat16)
    early_copies = []
    for step in range(1, groups):
        early_copies.append(
            remote(
                early_send.at[targets[step - 1]],
                early_slots.at[step - 1],
                early_send_sems.at[step - 1],
                early_recv_sems.at[step - 1],
                peers[2 + step],
            )
        )
    head_copy = remote(sent_ref, head_slot, single_send.at[0], single_recv.at[0], peers[2])
    side_copies = []
    for piece, owner in enumerate(order):
        core_copies[piece].wait()
        side_send[piece] = (
            late_ref[core, owner, 1 - side] + core_slot[piece, 1 - side]
        ).astype(jnp.bfloat16)
        side_copies.append(
            remote(
                side_send.at[piece],
                side_slot.at[piece],
                side_send_sems.at[piece],
                side_recv_sems.at[piece],
                peers[1],
            )
        )
        total[piece] = late_ref[core, owner, side] + core_slot[piece, side]
    late_copies = []
    for piece in range(groups):
        side_copies[piece].wait()
        total[piece] = total[piece] + side_slot[piece].astype(jnp.float32)
        if piece < groups - 1:
            late_send[piece] = total[piece].astype(jnp.bfloat16)
            late_copies.append(
                remote(
                    late_send.at[piece],
                    late_slots.at[piece],
                    late_send_sems.at[piece],
                    late_recv_sems.at[piece],
                    peers[3 + piece],
                )
            )
    head_copy.wait()
    summed_out[...] = kept_ref[...] + head_slot[...]
    result = early_ref[group]
    for step in range(1, groups):
        early_copies[step - 1].wait()
        result = result + early_slots[step - 1].astype(jnp.float32)
    early_out[...] = result
    result = total[groups - 1]
    for step in range(1, groups):
        late_copies[step - 1].wait()
        result = result + late_slots[step - 1].astype(jnp.float32)
    late_out[...] = result


def closing_sums(early, late, kept, sent):
    groups, rows, width = early.shape
    chunk = (groups, rows, width)
    slots = (groups - 1, rows, width)
    return pl.pallas_call(
        functools.partial(closing_kernel, groups),
        out_shape=(
            jax.ShapeDtypeStruct((rows, width), jnp.float32),
            jax.ShapeDtypeStruct((rows, width), jnp.float32),
            jax.ShapeDtypeStruct(kept.shape, jnp.float32),
        ),
        in_specs=[pl.BlockSpec(memory_space=pltpu.VMEM)] * 4,
        out_specs=[pl.BlockSpec(memory_space=pltpu.VMEM)] * 3,
        scratch_shapes=[
            pltpu.VMEM(chunk, jnp.bfloat16),
            pltpu.VMEM(slots, jnp.bfloat16),
            pltpu.VMEM((groups, 2, rows, width), jnp.float32),
            pltpu.VMEM(chunk, jnp.bfloat16),
            pltpu.VMEM(chunk, jnp.bfloat16),
            pltpu.VMEM(chunk, jnp.float32),
            pltpu.VMEM(chunk, jnp.bfloat16),
            pltpu.VMEM(slots, jnp.bfloat16),
            pltpu.VMEM(kept.shape, jnp.float32),
            pltpu.SemaphoreType.DMA((1,)),
            pltpu.SemaphoreType.DMA((1,)),
            pltpu.SemaphoreType.DMA((groups - 1,)),
            pltpu.SemaphoreType.DMA((groups - 1,)),
            pltpu.SemaphoreType.DMA((groups - 1,)),
            pltpu.SemaphoreType.DMA((groups - 1,)),
            pltpu.SemaphoreType.DMA((groups,)),
            pltpu.SemaphoreType.DMA((groups,)),
            pltpu.SemaphoreType.DMA((groups,)),
            pltpu.SemaphoreType.DMA((groups,)),
        ],
        compiler_params=pltpu.CompilerParams(
            collective_id=0, has_side_effects=True, vmem_limit_bytes=48 * 1024 * 1024
        ),
    )(early, late, kept, sent)


def body(
    embedded, grad_out, mask_pos, timestep, time_table, mask_embed, w_query, w_key, w_value, w_out
):
    seq_index = lax.axis_index("seq")
    seq_count = lax.axis_size("seq")
    head_place = lax.axis_index("head")
    core, side = seq_index % 2, seq_index // 2 % 2
    slab_rows = embedded.shape[0]
    total_len = slab_rows * seq_count
    scale = HEAD_DIM ** (-0.5)
    full_rows = joined_heads(embedded, head_place)
    full_grad = joined_heads(grad_out, head_place)
    positions = seq_index * slab_rows + jnp.arange(slab_rows, dtype=jnp.int32)
    masked = jnp.any(positions[:, None] == mask_pos[None, :], axis=1)
    time_row = lax.dynamic_slice_in_dim(time_table, timestep[0], 1, 0).astype(jnp.float32)
    hidden = (
        jnp.where(
            masked[:, None], mask_embed.astype(jnp.float32)[None, :], full_rows.astype(jnp.float32)
        )
        + time_row
    ).astype(jnp.bfloat16)
    key_rows = jnp.dot(hidden, w_key, preferred_element_type=jnp.float32).astype(jnp.bfloat16)
    value_rows = jnp.dot(hidden, w_value, preferred_element_type=jnp.float32).astype(jnp.bfloat16)
    queries = jnp.dot(hidden, w_query, preferred_element_type=jnp.float32).astype(jnp.bfloat16)
    grad_attn = contract_last(full_grad, w_out).astype(jnp.bfloat16)
    group_width = queries.shape[1]
    head_count = group_width // HEAD_DIM

    own = jnp.concatenate([key_rows, value_rows], axis=1)
    below = passed_along(own, "seq", 4)
    above = passed_along(own, "seq", -4)
    plane_side = swapped(own, "seq", 2)
    plane_core = swapped(own, "seq", 1)
    far_side = swapped(jnp.where(side == 1, below, above), "seq", 2)
    far_core = swapped(jnp.where(core == 1, below, above), "seq", 1)
    plane_both = swapped(plane_side, "seq", 1)
    far_both = swapped(far_side, "seq", 1)
    slabs = jnp.concatenate(
        [far_both, plane_both, far_core, plane_core, far_side, plane_side, own, below, above],
        axis=0,
    )
    core_step = 4 - 8 * (1 - core)
    side_step = 4 - 8 * (1 - side)
    numbers = [
        (seq_index ^ 3) + side_step,
        seq_index ^ 3,
        (seq_index ^ 1) + core_step,
        seq_index ^ 1,
        (seq_index ^ 2) + side_step,
        seq_index ^ 2,
        seq_index,
        seq_index - 4,
        seq_index + 4,
    ]
    offsets = jnp.arange(slab_rows, dtype=jnp.int32)
    key_pos = jnp.concatenate([number * slab_rows + offsets for number in numbers])
    keys_all = slabs[:, :group_width]
    values_all = slabs[:, group_width:]
    distance_grid = positions[:, None] - key_pos[None, :]
    band = (
        (jnp.abs(distance_grid) <= HALF) & (key_pos[None, :] >= 0) & (key_pos[None, :] < total_len)
    )
    head_outputs = []
    query_grads = []
    key_grads = []
    value_grads = []
    for head_index in range(head_count):
        lower_col = head_index * HEAD_DIM
        upper_col = lower_col + HEAD_DIM
        head_query = queries[:, lower_col:upper_col]
        head_keys = keys_all[:, lower_col:upper_col]
        head_values = values_all[:, lower_col:upper_col]
        head_grad = grad_attn[:, lower_col:upper_col]
        scores = contract_last(head_query, head_keys) * scale
        scores = jnp.where(band, scores, NEG_FILL)
        row_max = jnp.max(scores, axis=1, keepdims=True)
        log_total = row_max + jnp.log(jnp.sum(jnp.exp(scores - row_max), axis=1, keepdims=True))
        attention = jnp.exp(scores - log_total)
        rounded = attention.astype(jnp.bfloat16)
        output = jnp.dot(rounded, head_values, preferred_element_type=jnp.float32).astype(
            jnp.bfloat16
        )
        head_outputs.append(output)
        delta = jnp.sum(head_grad.astype(jnp.float32) * output.astype(jnp.float32), axis=1)
        dprob = contract_last(head_grad, head_values)
        dscore = (attention * (dprob - delta[:, None])).astype(jnp.bfloat16)
        query_grads.append(scale * jnp.dot(dscore, head_keys, preferred_element_type=jnp.float32))
        key_grads.append(scale * contract_first(head_query, dscore))
        value_grads.append(contract_first(head_grad, rounded))
    attn_out = jnp.concatenate(head_outputs, axis=1)
    query_rounded = jnp.concatenate(query_grads, axis=1).astype(jnp.bfloat16)
    slab_grads = jnp.concatenate(key_grads + value_grads, axis=0)

    def slab_of(first, count):
        return slab_grads[:, first * slab_rows : (first + count) * slab_rows]

    by_core = swapped(slab_of(0, 4), "seq", 1)
    for_side = (by_core[:, : 2 * slab_rows] + slab_of(4, 2)).astype(jnp.bfloat16)
    early_part = core_summed(
        [contract_first(hidden, query_rounded), contract_first(full_grad, attn_out)], seq_index
    )
    side_far = swapped(for_side[:, :slab_rows], "seq", 2)
    side_own = swapped(for_side[:, slab_rows:], "seq", 2).astype(jnp.float32)
    side_far, early_part = lax.optimization_barrier((side_far, early_part))
    side_far = side_far.astype(jnp.float32)
    early_part = side_summed(early_part, seq_index)
    core_far, core_own = by_core[:, 2 * slab_rows : 3 * slab_rows], by_core[:, 3 * slab_rows :]
    to_below = slab_of(7, 1) + jnp.where(core == 1, core_far, 0.0) + jnp.where(side == 1, side_far, 0.0)
    to_above = slab_of(8, 1) + jnp.where(core == 0, core_far, 0.0) + jnp.where(side == 0, side_far, 0.0)
    slab_total = slab_of(6, 1) + core_own + side_own
    slab_total = slab_total + passed_along(to_below.astype(jnp.bfloat16), "seq", -4).astype(jnp.float32)
    slab_total = slab_total + passed_along(to_above.astype(jnp.bfloat16), "seq", 4).astype(jnp.float32)
    pair_rounded = slab_total.astype(jnp.bfloat16)

    partial_grad = contract_last(query_rounded, w_query)
    partial_grad = partial_grad + contract_mixed(pair_rounded[:group_width], w_key)
    partial_grad = partial_grad + contract_mixed(pair_rounded[group_width:], w_value)
    half = embedded.shape[1]
    left, right = partial_grad[:, :half], partial_grad[:, half:]
    kept = jnp.where(head_place == 0, left, right)
    sent = jnp.where(head_place == 0, right, left)
    late_part = lax.dot_general(
        hidden, pair_rounded, (((0,), (1,)), ((), ())), preferred_element_type=jnp.float32
    )
    groups = seq_count // 4
    if groups > 4:
        early = group_summed(early_part)
        late = group_summed(side_summed(core_summed([late_part], seq_index), seq_index))
        summed = kept + swapped(sent, "head", 1)
    else:
        rows = late_part.shape[0] // seq_count
        blocks = late_part.reshape(groups, 2, 2, rows, late_part.shape[1]).transpose(2, 0, 1, 3, 4)
        early, late, summed = closing_sums(early_part, blocks, kept, sent)
    input_grad = jnp.where(masked[:, None], 0.0, summed).astype(jnp.bfloat16)
    return (
        input_grad,
        early[:, :group_width],
        late[:, :group_width],
        late[:, group_width:],
        early[:, group_width:],
    )


def solution(mesh):
    placed = (
        P("seq", "head"),
        P("seq", "head"),
        P("seq"),
        P(),
        P(),
        P(),
        P(None, "head"),
        P(None, "head"),
        P(None, "head"),
        P("head", None),
    )
    return jax.shard_map(
        body,
        mesh=mesh,
        in_specs=placed,
        out_specs=(
            P("seq", "head"),
            P("seq", "head"),
            P("seq", "head"),
            P("seq", "head"),
            P("seq", "head"),
        ),
        check_vma=False,
    )
```

```python
import functools

import jax
import jax.numpy as jnp
from jax import lax
from jax.experimental import pallas as pl
from jax.experimental.pallas import tpu as pltpu
from jax.sharding import PartitionSpec as P

HEAD_DIM = 64
HALF = 1024


NEG_FILL = -1e30


def contract_first(left, right):
    return lax.dot_general(
        left, right, (((0,), (0,)), ((), ())), preferred_element_type=jnp.float32
    )


def contract_last(left, right):
    return lax.dot_general(
        left, right, (((1,), (1,)), ((), ())), preferred_element_type=jnp.float32
    )


def contract_mixed(left, right):
    return lax.dot_general(
        left, right, (((0,), (1,)), ((), ())), preferred_element_type=jnp.float32
    )


def swapped(value, axis, bit):
    count = lax.axis_size(axis)
    return lax.ppermute(value, axis, [(source, source ^ bit) for source in range(count)])


def passed_along(value, axis, steps):
    count = lax.axis_size(axis)
    first, last = (max(0, -steps), min(count, count - steps))
    return lax.ppermute(value, axis, [(source, source + steps) for source in range(first, last)])


def picked(array, index, axis):
    return lax.dynamic_index_in_dim(array, index, axis, keepdims=False)


def joined_heads(mine, head_index):
    other = swapped(mine, "head", 1)
    first = jnp.where(head_index == 0, mine, other)
    second = jnp.where(head_index == 0, other, mine)
    return jnp.concatenate([first, second], axis=1)


def core_summed(parts, seq_index):
    count = lax.axis_size("seq")
    core = seq_index % 2
    blocks = [part.reshape(count // 4, 2, 2, -1, part.shape[1]) for part in parts]
    kept = jnp.concatenate([picked(block, core, 2) for block in blocks], axis=3)
    sent = jnp.concatenate([picked(block, 1 - core, 2) for block in blocks], axis=3)
    return kept + swapped(sent, "seq", 1)


def side_summed(blocks, seq_index):
    side = seq_index // 2 % 2
    sent = picked(blocks, 1 - side, 1).astype(jnp.bfloat16)
    return picked(blocks, side, 1) + swapped(sent, "seq", 2).astype(jnp.float32)


def group_summed(blocks):
    groups, rows, width = blocks.shape
    members = [[g * 4 + place for g in range(groups)] for place in range(4)]
    return lax.psum_scatter(
        blocks.reshape(groups * rows, width),
        "seq",
        scatter_dimension=0,
        axis_index_groups=members,
        tiled=True,
    )


def closing_kernel(
    groups,
    early_ref,
    late_ref,
    kept_ref,
    sent_ref,
    early_out,
    late_out,
    summed_out,
    early_send,
    early_slots,
    core_slot,
    side_send,
    side_slot,
    total,
    late_send,
    late_slots,
    head_slot,
    single_send,
    single_recv,
    early_send_sems,
    early_recv_sems,
    late_send_sems,
    late_recv_sems,
    core_send_sems,
    core_recv_sems,
    side_send_sems,
    side_recv_sems,
):
    me = lax.axis_index("seq")
    head = lax.axis_index("head")
    core = lax.rem(me, 2)
    side = lax.rem(me // 2, 2)
    group = me // 4
    place = lax.rem(me, 4)
    core_peer = me + 1 - 2 * core
    side_peer = me + 2 - 4 * side
    targets = [lax.rem(group + step, groups) for step in range(1, groups)]
    peers = [(core_peer, head), (side_peer, head), (me, 1 - head)]
    peers += [(target * 4 + place, head) for target in targets]

    barrier = pltpu.get_barrier_semaphore()
    for peer in peers:
        pl.semaphore_signal(barrier, inc=1, device_id=peer, device_id_type=pl.DeviceIdType.MESH)
    pl.semaphore_wait(barrier, len(peers))

    def remote(source, target, send, recv, peer):
        copy = pltpu.make_async_remote_copy(
            src_ref=source,
            dst_ref=target,
            send_sem=send,
            recv_sem=recv,
            device_id=peer,
            device_id_type=pl.DeviceIdType.MESH,
        )
        copy.start()
        return copy

    order = targets + [group]
    core_copies = []
    for piece, owner in enumerate(order):
        core_copies.append(
            remote(
                late_ref.at[1 - core, owner],
                core_slot.at[piece],
                core_send_sems.at[piece],
                core_recv_sems.at[piece],
                peers[0],
            )
        )
    early_send[...] = early_ref[...].astype(jnp.bfloat16)
    early_copies = []
    for step in range(1, groups):
        early_copies.append(
            remote(
                early_send.at[targets[step - 1]],
                early_slots.at[step - 1],
                early_send_sems.at[step - 1],
                early_recv_sems.at[step - 1],
                peers[2 + step],
            )
        )
    head_copy = remote(sent_ref, head_slot, single_send.at[0], single_recv.at[0], peers[2])
    side_copies = []
    for piece, owner in enumerate(order):
        core_copies[piece].wait()
        side_send[piece] = (
            late_ref[core, owner, 1 - side] + core_slot[piece, 1 - side]
        ).astype(jnp.bfloat16)
        side_copies.append(
            remote(
                side_send.at[piece],
                side_slot.at[piece],
                side_send_sems.at[piece],
                side_recv_sems.at[piece],
                peers[1],
            )
        )
        total[piece] = late_ref[core, owner, side] + core_slot[piece, side]
    late_copies = []
    for piece in range(groups):
        side_copies[piece].wait()
        total[piece] = total[piece] + side_slot[piece].astype(jnp.float32)
        if piece < groups - 1:
            late_send[piece] = total[piece].astype(jnp.bfloat16)
            late_copies.append(
                remote(
                    late_send.at[piece],
                    late_slots.at[piece],
                    late_send_sems.at[piece],
                    late_recv_sems.at[piece],
                    peers[3 + piece],
                )
            )
    head_copy.wait()
    summed_out[...] = kept_ref[...] + head_slot[...]
    result = early_ref[group]
    for step in range(1, groups):
        early_copies[step - 1].wait()
        result = result + early_slots[step - 1].astype(jnp.float32)
    early_out[...] = result
    result = total[groups - 1]
    for step in range(1, groups):
        late_copies[step - 1].wait()
        result = result + late_slots[step - 1].astype(jnp.float32)
    late_out[...] = result


def closing_sums(early, late, kept, sent):
    groups, rows, width = early.shape
    chunk = (groups, rows, width)
    slots = (groups - 1, rows, width)
    return pl.pallas_call(
        functools.partial(closing_kernel, groups),
        out_shape=(
            jax.ShapeDtypeStruct((rows, width), jnp.float32),
            jax.ShapeDtypeStruct((rows, width), jnp.float32),
            jax.ShapeDtypeStruct(kept.shape, jnp.float32),
        ),
        in_specs=[pl.BlockSpec(memory_space=pltpu.VMEM)] * 4,
        out_specs=[pl.BlockSpec(memory_space=pltpu.VMEM)] * 3,
        scratch_shapes=[
            pltpu.VMEM(chunk, jnp.bfloat16),
            pltpu.VMEM(slots, jnp.bfloat16),
            pltpu.VMEM((groups, 2, rows, width), jnp.float32),
            pltpu.VMEM(chunk, jnp.bfloat16),
            pltpu.VMEM(chunk, jnp.bfloat16),
            pltpu.VMEM(chunk, jnp.float32),
            pltpu.VMEM(chunk, jnp.bfloat16),
            pltpu.VMEM(slots, jnp.bfloat16),
            pltpu.VMEM(kept.shape, jnp.float32),
            pltpu.SemaphoreType.DMA((1,)),
            pltpu.SemaphoreType.DMA((1,)),
            pltpu.SemaphoreType.DMA((groups - 1,)),
            pltpu.SemaphoreType.DMA((groups - 1,)),
            pltpu.SemaphoreType.DMA((groups - 1,)),
            pltpu.SemaphoreType.DMA((groups - 1,)),
            pltpu.SemaphoreType.DMA((groups,)),
            pltpu.SemaphoreType.DMA((groups,)),
            pltpu.SemaphoreType.DMA((groups,)),
            pltpu.SemaphoreType.DMA((groups,)),
        ],
        compiler_params=pltpu.CompilerParams(
            collective_id=0, has_side_effects=True, vmem_limit_bytes=48 * 1024 * 1024
        ),
    )(early, late, kept, sent)


def body(
    embedded, grad_out, mask_pos, timestep, time_table, mask_embed, w_query, w_key, w_value, w_out
):
    seq_index = lax.axis_index("seq")
    seq_count = lax.axis_size("seq")
    head_place = lax.axis_index("head")
    core, side = seq_index % 2, seq_index // 2 % 2
    slab_rows = embedded.shape[0]
    total_len = slab_rows * seq_count
    scale = HEAD_DIM ** (-0.5)
    full_rows = joined_heads(embedded, head_place)
    full_grad = joined_heads(grad_out, head_place)
    positions = seq_index * slab_rows + jnp.arange(slab_rows, dtype=jnp.int32)
    masked = jnp.any(positions[:, None] == mask_pos[None, :], axis=1)
    time_row = lax.dynamic_slice_in_dim(time_table, timestep[0], 1, 0).astype(jnp.float32)
    hidden = (
        jnp.where(
            masked[:, None], mask_embed.astype(jnp.float32)[None, :], full_rows.astype(jnp.float32)
        )
        + time_row
    ).astype(jnp.bfloat16)
    key_rows = jnp.dot(hidden, w_key, preferred_element_type=jnp.float32).astype(jnp.bfloat16)
    value_rows = jnp.dot(hidden, w_value, preferred_element_type=jnp.float32).astype(jnp.bfloat16)
    queries = jnp.dot(hidden, w_query, preferred_element_type=jnp.float32).astype(jnp.bfloat16)
    grad_attn = contract_last(full_grad, w_out).astype(jnp.bfloat16)
    group_width = queries.shape[1]
    head_count = group_width // HEAD_DIM

    own = jnp.concatenate([key_rows, value_rows], axis=1)
    below = passed_along(own, "seq", 4)
    above = passed_along(own, "seq", -4)
    plane_side = swapped(own, "seq", 2)
    plane_core = swapped(own, "seq", 1)
    far_side = swapped(jnp.where(side == 1, below, above), "seq", 2)
    far_core = swapped(jnp.where(core == 1, below, above), "seq", 1)
    plane_both = swapped(plane_side, "seq", 1)
    far_both = swapped(far_side, "seq", 1)
    slabs = jnp.concatenate(
        [far_both, plane_both, far_core, plane_core, far_side, plane_side, own, below, above],
        axis=0,
    )
    core_step = 4 - 8 * (1 - core)
    side_step = 4 - 8 * (1 - side)
    numbers = [
        (seq_index ^ 3) + side_step,
        seq_index ^ 3,
        (seq_index ^ 1) + core_step,
        seq_index ^ 1,
        (seq_index ^ 2) + side_step,
        seq_index ^ 2,
        seq_index,
        seq_index - 4,
        seq_index + 4,
    ]
    offsets = jnp.arange(slab_rows, dtype=jnp.int32)
    key_pos = jnp.concatenate([number * slab_rows + offsets for number in numbers])
    keys_all = slabs[:, :group_width]
    values_all = slabs[:, group_width:]
    distance_grid = positions[:, None] - key_pos[None, :]
    band = (
        (jnp.abs(distance_grid) <= HALF) & (key_pos[None, :] >= 0) & (key_pos[None, :] < total_len)
    )
    head_outputs = []
    query_grads = []
    key_grads = []
    value_grads = []
    for head_index in range(head_count):
        lower_col = head_index * HEAD_DIM
        upper_col = lower_col + HEAD_DIM
        head_query = queries[:, lower_col:upper_col]
        head_keys = keys_all[:, lower_col:upper_col]
        head_values = values_all[:, lower_col:upper_col]
        head_grad = grad_attn[:, lower_col:upper_col]
        scores = contract_last(head_query, head_keys) * scale
        scores = jnp.where(band, scores, NEG_FILL)
        row_max = jnp.max(scores, axis=1, keepdims=True)
        log_total = row_max + jnp.log(jnp.sum(jnp.exp(scores - row_max), axis=1, keepdims=True))
        attention = jnp.exp(scores - log_total)
        rounded = attention.astype(jnp.bfloat16)
        output = jnp.dot(rounded, head_values, preferred_element_type=jnp.float32).astype(
            jnp.bfloat16
        )
        head_outputs.append(output)
        delta = jnp.sum(head_grad.astype(jnp.float32) * output.astype(jnp.float32), axis=1)
        dprob = contract_last(head_grad, head_values)
        dscore = (attention * (dprob - delta[:, None])).astype(jnp.bfloat16)
        query_grads.append(scale * jnp.dot(dscore, head_keys, preferred_element_type=jnp.float32))
        key_grads.append(scale * contract_first(head_query, dscore))
        value_grads.append(contract_first(head_grad, rounded))
    attn_out = jnp.concatenate(head_outputs, axis=1)
    query_rounded = jnp.concatenate(query_grads, axis=1).astype(jnp.bfloat16)
    slab_grads = jnp.concatenate(key_grads + value_grads, axis=0)

    def slab_of(first, count):
        return slab_grads[:, first * slab_rows : (first + count) * slab_rows]

    by_core = swapped(slab_of(0, 4), "seq", 1)
    for_side = (by_core[:, : 2 * slab_rows] + slab_of(4, 2)).astype(jnp.bfloat16)
    for_side, query_rounded, attn_out = lax.optimization_barrier(
        (for_side, query_rounded, attn_out)
    )
    early_part = core_summed(
        [contract_first(hidden, query_rounded), contract_first(full_grad, attn_out)], seq_index
    )
    by_side, early_part = lax.optimization_barrier((swapped(for_side, "seq", 2), early_part))
    by_side = by_side.astype(jnp.float32)
    early_part = side_summed(early_part, seq_index)
    core_far, core_own = by_core[:, 2 * slab_rows : 3 * slab_rows], by_core[:, 3 * slab_rows :]
    side_far, side_own = by_side[:, :slab_rows], by_side[:, slab_rows:]
    to_below = slab_of(7, 1) + jnp.where(core == 1, core_far, 0.0) + jnp.where(side == 1, side_far, 0.0)
    to_above = slab_of(8, 1) + jnp.where(core == 0, core_far, 0.0) + jnp.where(side == 0, side_far, 0.0)
    slab_total = slab_of(6, 1) + core_own + side_own
    slab_total = slab_total + passed_along(to_below.astype(jnp.bfloat16), "seq", -4).astype(jnp.float32)
    slab_total = slab_total + passed_along(to_above.astype(jnp.bfloat16), "seq", 4).astype(jnp.float32)
    pair_rounded = slab_total.astype(jnp.bfloat16)

    partial_grad = contract_last(query_rounded, w_query)
    partial_grad = partial_grad + contract_mixed(pair_rounded[:group_width], w_key)
    partial_grad = partial_grad + contract_mixed(pair_rounded[group_width:], w_value)
    half = embedded.shape[1]
    left, right = partial_grad[:, :half], partial_grad[:, half:]
    kept = jnp.where(head_place == 0, left, right)
    sent = jnp.where(head_place == 0, right, left)
    late_part = lax.dot_general(
        hidden, pair_rounded, (((0,), (1,)), ((), ())), preferred_element_type=jnp.float32
    )
    groups = seq_count // 4
    if groups > 4:
        early = group_summed(early_part)
        late = group_summed(side_summed(core_summed([late_part], seq_index), seq_index))
        summed = kept + swapped(sent, "head", 1)
    else:
        rows = late_part.shape[0] // seq_count
        blocks = late_part.reshape(groups, 2, 2, rows, late_part.shape[1]).transpose(2, 0, 1, 3, 4)
        early, late, summed = closing_sums(early_part, blocks, kept, sent)
    input_grad = jnp.where(masked[:, None], 0.0, summed).astype(jnp.bfloat16)
    return (
        input_grad,
        early[:, :group_width],
        late[:, :group_width],
        late[:, group_width:],
        early[:, group_width:],
    )


def solution(mesh):
    placed = (
        P("seq", "head"),
        P("seq", "head"),
        P("seq"),
        P(),
        P(),
        P(),
        P(None, "head"),
        P(None, "head"),
        P(None, "head"),
        P("head", None),
    )
    return jax.shard_map(
        body,
        mesh=mesh,
        in_specs=placed,
        out_specs=(
            P("seq", "head"),
            P("seq", "head"),
            P("seq", "head"),
            P("seq", "head"),
            P("seq", "head"),
        ),
        check_vma=False,
    )
```
